32 devices in a mesh: dp: 8 (over y, x, core), tensor: 4 (over z).
Axes of the slice: x: 2, y: 2, z: 4, core: 2. Of those that a mesh axis runs over, the one named last changes fastest.
Arguments:
- tokens: bfloat16 [580, 8, 1024], P('tensor', 'dp'), may hold values from -6 to 6
- ln1_gain: bfloat16 [1024], P('dp'), may hold values from 0.099609375 to 1.8984375
- ln1_bias: bfloat16 [1024], P('dp'), may hold values from -1.5 to 1.5
- w_qkv: bfloat16 [3, 1024, 1024], P(None, 'dp', 'tensor'), may hold values from -0.1875 to 0.1875
- b_qv: bfloat16 [2, 1024], P(None, 'dp'), may hold values from -1.5 to 1.5
- w_out: bfloat16 [1024, 1024], P('tensor', 'dp'), may hold values from -0.75 to 0.75
- b_out: bfloat16 [1024], P('dp'), may hold values from -1.5 to 1.5
- ln2_gain: bfloat16 [1024], P('dp'), may hold values from 0.099609375 to 1.8984375
- ln2_bias: bfloat16 [1024], P('dp'), may hold values from -1.5 to 1.5
- w_up: bfloat16 [1024, 4096], P('dp', 'tensor'), may hold values from -0.1875 to 0.1875
- b_up: bfloat16 [4096], P('dp'), may hold values from -2.5 to 2.5
- w_down: bfloat16 [4096, 1024], P('tensor', 'dp'), may hold values from -0.09375 to 0.09375
- b_down: bfloat16 [1024], P('dp'), may hold values from -1.5 to 1.5
- cotangent: bfloat16 [580, 8, 1024], P('tensor', 'dp'), may hold values from -6 to 6
Outputs:
- mixed: bfloat16 [580, 8, 1024], P('tensor', 'dp')
- grad_tokens: float32 [580, 8, 1024], P('tensor', 'dp')
- grad_ln1_gain: float32 [1024], P('dp')
- grad_ln1_bias: float32 [1024], P('dp')
- grad_w_qkv: float32 [3, 1024, 1024], P(None, 'dp', 'tensor')
- grad_b_qv: float32 [2, 1024], P(None, 'dp')
- grad_w_out: float32 [1024, 1024], P('tensor', 'dp')
- grad_b_out: float32 [1024], P('dp')
- grad_ln2_gain: float32 [1024], P('dp')
- grad_ln2_bias: float32 [1024], P('dp')
- grad_w_up: float32 [1024, 4096], P('dp', 'tensor')
- grad_b_up: float32 [4096], P('dp')
- grad_w_down: float32 [4096, 1024], P('tensor', 'dp')
- grad_b_down: float32 [1024], P('dp')
The draws below stay inside these ranges and needn't reach their ends.
All inputs are finite; a program needn't handle non-finite values.
Results may differ from the reference program's by a relative error of at most 0.017.
Values may be sent and summed in bfloat16 or wider, within the bound.
A program may use at most 128 MiB of HBM per device.

```python
from functools import partial
import jax
import jax.numpy as jnp
from jax import lax

D = 1024
HEADS = 16
HEAD_DIM = 64
FF = 4096
SEQ = 577
PADDED = 580
IMAGES = 8


def steps_of(key, shape, cuts, smallest, largest):
    level = 1.0
    for dim, blocks in cuts:
        heights = jax.random.uniform(jax.random.fold_in(jax.random.fold_in(key, 6), dim), (blocks,), jnp.float32, smallest / len(cuts), largest / len(cuts))
        level = level * jnp.repeat(jnp.exp(heights), shape[dim] // blocks).reshape((-1,) + (1,) * (len(shape) - 1 - dim))
    return level


def noise(rng, dims, width, most, pieces=(), kind=jnp.bfloat16):
    level = steps_of(rng, dims, pieces, -0.22, 0.18) if pieces else 1.0
    values = jax.random.normal(rng, dims, jnp.float32) * width * level
    return jnp.minimum(jnp.maximum(values, -most), most).astype(kind)


def setup_inputs(seed: int = 0) -> dict:
    key_list = jax.random.split(jax.random.key(seed), 15)
    tokens = noise(key_list[0], (PADDED, IMAGES, D), 1.0, 6.0, ((0, 4), (1, 8)))
    ln1_gain = jnp.clip(1.0 + 0.18 * jax.random.normal(key_list[1], (D,), jnp.float32), 0.099609375, 1.8984375).astype(jnp.bfloat16)
    ln1_bias = noise(key_list[2], (D,), 0.3, 1.5, ((0, 8),))
    w_qkv = noise(key_list[3], (3, D, D), D ** -0.5, 0.1875, ((1, 8), (2, 4)))
    b_qv = noise(key_list[4], (2, D), 0.3, 1.5, ((1, 8),))
    w_out = noise(key_list[5], (D, D), (D // 16) ** -0.5, 0.75, ((0, 4), (1, 8)))
    b_out = noise(key_list[6], (D,), 0.3, 1.5, ((0, 8),))
    ln2_gain = jnp.clip(1.0 + 0.18 * jax.random.normal(key_list[7], (D,), jnp.float32), 0.099609375, 1.8984375).astype(jnp.bfloat16)
    ln2_bias = noise(key_list[8], (D,), 0.3, 1.5, ((0, 8),))
    w_up = noise(key_list[9], (D, FF), D ** -0.5, 0.1875, ((0, 8), (1, 4)))
    b_up = noise(key_list[10], (FF,), 0.5, 2.5, ((0, 8),))
    w_down = noise(key_list[11], (FF, D), FF ** -0.5, 0.09375, ((0, 4), (1, 8)))
    b_down = noise(key_list[12], (D,), 0.3, 1.5, ((0, 8),))
    cotangent = noise(key_list[13], (PADDED, IMAGES, D), 1.0, 6.0, ((0, 4), (1, 8)))
    return {"tokens": tokens, "ln1_gain": ln1_gain, "ln1_bias": ln1_bias, "w_qkv": w_qkv, "b_qv": b_qv, "w_out": w_out, "b_out": b_out, "ln2_gain": ln2_gain, "ln2_bias": ln2_bias, "w_up": w_up, "b_up": b_up, "w_down": w_down, "b_down": b_down, "cotangent": cotangent}


@jax.custom_vjp
def low(v):
    return lax.optimization_barrier(v.astype(jnp.bfloat16)).astype(jnp.float32)

@jax.custom_vjp
def low_back(v):
    return v

def low_keep(v):
    return (low(v), None)

def low_pass(kept, grad):
    return (grad,)

def back_keep(v):
    return (v, None)

def back_low(kept, grad):
    return (low(grad),)
low.defvjp(low_keep, low_pass)
low_back.defvjp(back_keep, back_low)
EPS = 1e-06
NEG = -1000000000.0

def layer_norm(values, gain, shift):
    center = values - lax.optimization_barrier(jnp.mean(values, axis=-1, keepdims=True))
    spread = lax.optimization_barrier(jnp.mean(center * center, axis=-1, keepdims=True))
    return center * lax.rsqrt(spread + EPS) * gain + shift

def matmul(left, right):
    return jnp.dot(left, right, precision=lax.Precision.HIGHEST, preferred_element_type=jnp.float32)

def one_image(image, params):
    gain_one, shift_one, w_qkv, b_qv, w_out, b_out, gain_two, shift_two, w_up, b_up, w_down, b_down = params
    total = image.shape[0]
    normed = low(layer_norm(image, gain_one, shift_one))
    queries = low(low_back(matmul(normed, w_qkv[0]) + b_qv[0]))
    keys = low(low_back(matmul(normed, w_qkv[1])))
    values = low(low_back(matmul(normed, w_qkv[2]) + b_qv[1]))
    split_q = queries.reshape(total, HEADS, HEAD_DIM)
    split_k = keys.reshape(total, HEADS, HEAD_DIM)
    split_v = values.reshape(total, HEADS, HEAD_DIM)
    scale = 1.0 / jnp.sqrt(jnp.float32(HEAD_DIM))
    scores = low_back(jnp.einsum('qhe,khe->hqk', split_q, split_k, precision=lax.Precision.HIGHEST) * scale)
    live = jnp.arange(total, dtype=jnp.int32) < SEQ
    scores = jnp.where(live[None, None, :], scores, NEG)
    probs = jax.nn.softmax(scores, axis=-1)
    heads = jnp.einsum('hqk,khe->qhe', low(probs), split_v, precision=lax.Precision.HIGHEST).reshape(total, D)
    heads = low(low_back(heads))
    branch = low_back(matmul(heads, w_out) + b_out)
    first = image + branch
    normed_two = low(layer_norm(first, gain_two, shift_two))
    pre_act = low_back(matmul(normed_two, w_up) + b_up)
    activated = low(jax.nn.gelu(pre_act, approximate=False))
    return first + matmul(activated, w_down) + b_down

def forward(inputs, *params):
    per_image = jnp.moveaxis(inputs, 1, 0)
    result = lax.map(jax.checkpoint(partial(one_image, params=params)), per_image)
    return jnp.moveaxis(result, 0, 1)

def reference(tokens, ln1_gain, ln1_bias, w_qkv, b_qv, w_out, b_out, ln2_gain, ln2_bias, w_up, b_up, w_down, b_down, cotangent):
    params = [p.astype(jnp.float32) for p in (ln1_gain, ln1_bias, w_qkv, b_qv, w_out, b_out, ln2_gain, ln2_bias, w_up, b_up, w_down, b_down)]
    inputs = tokens.astype(jnp.float32)
    live = (jnp.arange(tokens.shape[0], dtype=jnp.int32) < SEQ)[:, None, None]
    masked_grad = jnp.where(live, cotangent.astype(jnp.float32), jnp.float32(0.0))
    output, pull = jax.vjp(forward, inputs, *params)
    grads = pull(masked_grad)
    return (output.astype(jnp.bfloat16), grads[0], grads[1], grads[2], grads[3], grads[4], grads[5], grads[6], grads[7], grads[8], grads[9], grads[10], grads[11], grads[12])
```

```python
import math

import jax
import jax.numpy as jnp
from jax import lax
from jax.experimental import pallas as pl
from jax.experimental.pallas import tpu as pltpu
from jax.sharding import PartitionSpec as P

HEAD_DIM = 64
SEQ = 577
EPS = 1e-06
NEG = -1000000000.0
MESH = pl.DeviceIdType.MESH
LANES = 128


def at_dim(dim, size):
    def view(ref, j):
        start = pl.multiple_of(j * size, size)
        index = [slice(None)] * len(ref.shape)
        index[dim] = pl.ds(start, size)
        return ref.at[tuple(index)]

    return view


def at_front(ref, j):
    return ref.at[j]


def loop(first, last, step):
    def run(k, carry):
        step(k)
        return carry

    lax.fori_loop(first, last, run, 0)


class Item:
    def __init__(self, kind, array, out_shape, src, dst):
        self.kind, self.array, self.src, self.dst = kind, array, src, dst
        self.out = jax.ShapeDtypeStruct(out_shape, array.dtype)


def whole(ref, j):
    return ref


def gather_tensor(array):
    n = lax.axis_size("tensor")
    return Item("tensor", array, (n, *array.shape), whole, at_front)


def swap_tensor(array):
    return Item("tensor", array, array.shape, at_front, at_front)


def gather_dp(array, dim):
    n = lax.axis_size("dp")
    size = array.shape[dim]
    if dim == array.ndim - 1 and size % LANES:
        return Item("gather", array, (n, *array.shape), whole, at_front)
    shape = list(array.shape)
    shape[dim] *= n
    return Item("gather", array, tuple(shape), whole, at_dim(dim, size))


def joined(value, dim):
    if value.ndim == 2:
        return value
    moved = jnp.moveaxis(value, 0, dim)
    return moved.reshape(*moved.shape[:dim], -1, *moved.shape[dim + 2 :])


def swap_dp(array, dim):
    n = lax.axis_size("dp")
    size = array.shape[dim] // n
    shape = list(array.shape)
    shape[dim] = size
    if dim == array.ndim - 1 and size % LANES:
        parts = array.reshape(*array.shape[:dim], n, size)
        parts = jnp.moveaxis(parts, dim, 0)
        return Item("swap", parts, parts.shape, at_front, at_front)
    return Item("swap", array, (n, *shape), at_dim(dim, size), at_front)


def exchange(name, number, items):
    count = len(items)
    n_t = lax.axis_size("tensor")
    n_dp = lax.axis_size("dp")
    chips = n_dp // 2
    with_tensor = any(i.kind == "tensor" for i in items)
    with_gather = any(i.kind == "gather" for i in items)
    with_swap = any(i.kind == "swap" for i in items)

    def kernel(*refs):
        srcs = refs[:count]
        dsts = refs[count : 2 * count]
        own_sem, send, recv, fsend, frecv, ssend, srecv, tsend, trecv = refs[2 * count :]
        t = lax.axis_index("tensor")
        d = lax.axis_index("dp")
        core = lax.rem(d, 2)
        chip = d // 2
        sibling = d + 1 - 2 * core
        barrier = pltpu.get_barrier_semaphore()

        def hello(dp_id, t_id):
            pl.semaphore_signal(
                barrier, inc=1, device_id=(dp_id, t_id), device_id_type=MESH
            )

        def same_core(k):
            return lax.rem(chip + k, chips) * 2 + core

        greeted = 0
        if with_tensor:
            for k in range(1, n_t):
                hello(d, lax.rem(t + k, n_t))
            greeted += n_t - 1
        if with_swap:
            loop(1, n_dp, lambda k: hello(lax.rem(d + k, n_dp), t))
            greeted += n_dp - 1
        elif with_gather:
            loop(1, chips, lambda k: hello(same_core(k), t))
            hello(sibling, t)
            greeted += chips
        pl.semaphore_wait(barrier, greeted)

        def remote(src, dst, ssem, rsem, dp_id, t_id):
            return pltpu.make_async_remote_copy(
                src_ref=src,
                dst_ref=dst,
                send_sem=ssem,
                recv_sem=rsem,
                device_id=(dp_id, t_id),
                device_id_type=MESH,
            )

        def tensor_copy(i, k, owner):
            to = lax.rem(t + k, n_t)
            return remote(
                items[i].src(srcs[i], to),
                items[i].dst(dsts[i], owner),
                tsend.at[i, k],
                trecv.at[i, k],
                d,
                to,
            )

        def swap_copy(i, k, owner):
            to = lax.rem(d + k, n_dp)
            return remote(
                items[i].src(srcs[i], to),
                items[i].dst(dsts[i], owner),
                ssend.at[i, k],
                srecv.at[i, k],
                to,
                t,
            )

        def gather_copy(i, k, owner):
            return remote(
                srcs[i],
                items[i].dst(dsts[i], owner),
                send.at[i, k],
                recv.at[i, k],
                same_core(k),
                t,
            )

        def forward_copy(i, k, owner, own):
            block = items[i].dst(dsts[i], owner)
            return remote(
                srcs[i] if own else block, block, fsend.at[i, k], frecv.at[i, k], sibling, t
            )

        def own_copy(i):
            me = t if items[i].kind == "tensor" else d
            return pltpu.make_async_copy(
                items[i].src(srcs[i], me), items[i].dst(dsts[i], me), own_sem.at[i]
            )

        def of(kind):
            return [i for i in range(count) if items[i].kind == kind]

        for k in (2, 3, 1) if n_t == 4 else range(1, n_t):
            for i in of("tensor"):
                tensor_copy(i, k, t).start()
        for i in of("gather"):
            loop(1, chips, lambda k, i=i: gather_copy(i, k, d).start())
            forward_copy(i, 0, d, True).start()
        for i in of("swap"):
            loop(1, n_dp, lambda k, i=i: swap_copy(i, k, d).start())
        for i in range(count):
            own_copy(i).start()

        def came(k):
            return lax.rem(chip + chips - k, chips) * 2

        for i in of("gather"):

            def pass_on(k, i=i):
                gather_copy(i, k, came(k) + core).wait_recv()
                forward_copy(i, k, came(k) + core, False).start()

            loop(1, chips, pass_on)
        for i in of("gather"):
            other = 1 - core
            forward_copy(i, 0, came(0) + other, True).wait_recv()
            forward_copy(i, 0, d, True).wait_send()

            def finish(k, i=i):
                forward_copy(i, k, came(k) + other, False).wait_recv()
                forward_copy(i, k, came(k) + core, False).wait_send()
                gather_copy(i, k, d).wait_send()

            loop(1, chips, finish)
        for i in of("swap"):

            def end(k, i=i):
                swap_copy(i, k, lax.rem(d + n_dp - k, n_dp)).wait_recv()
                swap_copy(i, k, d).wait_send()

            loop(1, n_dp, end)
        for i in of("tensor"):
            for k in range(1, n_t):
                tensor_copy(i, k, lax.rem(t + n_t - k, n_t)).wait_recv()
                tensor_copy(i, k, t).wait_send()
        for i in range(count):
            own_copy(i).wait()

    dma = pltpu.SemaphoreType.DMA
    sent = sum(math.prod(i.out.shape) * i.out.dtype.itemsize for i in items)
    return pl.pallas_call(
        kernel,
        out_shape=tuple(i.out for i in items),
        in_specs=[pl.BlockSpec(memory_space=pl.ANY)] * count,
        out_specs=tuple([pl.BlockSpec(memory_space=pl.ANY)] * count),
        scratch_shapes=[
            dma((count,)),
            dma((count, chips)),
            dma((count, chips)),
            dma((count, chips)),
            dma((count, chips)),
            dma((count, n_dp)),
            dma((count, n_dp)),
            dma((count, n_t)),
            dma((count, n_t)),
        ],
        compiler_params=pltpu.CompilerParams(collective_id=number, has_side_effects=True),
        cost_estimate=pl.CostEstimate(flops=0, bytes_accessed=2 * sent, transcendentals=0),
        name=name,
    )(*(i.array for i in items))


def layer_norm(values, gain, shift):
    center = values - jnp.mean(values, axis=-1, keepdims=True)
    spread = jnp.mean(center * center, axis=-1, keepdims=True)
    return center * lax.rsqrt(spread + EPS) * gain + shift


def normalized(values):
    center = values - jnp.mean(values, axis=-1, keepdims=True)
    scale = lax.rsqrt(jnp.mean(center * center, axis=-1, keepdims=True) + EPS)
    return center * scale, scale


def norm_back(grad, gain, hat, scale):
    inner = grad * gain
    mean = jnp.mean(inner, axis=-1, keepdims=True)
    along = jnp.mean(inner * hat, axis=-1, keepdims=True)
    return (inner - mean - hat * along) * scale


def exact_gelu(values):
    return jax.nn.gelu(values, approximate=False)


def summed(parts):
    return jnp.sum(parts.astype(jnp.float32), axis=0)


def body(
    tokens,
    ln1_gain,
    ln1_bias,
    w_qkv,
    b_qv,
    w_out,
    b_out,
    ln2_gain,
    ln2_bias,
    w_up,
    b_up,
    w_down,
    b_down,
    cotangent,
):
    f32, bf16 = jnp.float32, jnp.bfloat16
    slot, images, width = tokens.shape
    parts = lax.axis_size("tensor")
    n_dp = lax.axis_size("dp")
    member = lax.axis_index("tensor")
    padded = -(-slot // 16) * 16
    total = padded * parts
    row = jnp.arange(padded, dtype=jnp.int32)
    at = (jnp.arange(parts, dtype=jnp.int32)[:, None] * slot + row[None, :]).reshape(total)
    key_live = (at < SEQ) & (jnp.tile(row, parts) < slot)
    own_live = (member * slot + jnp.arange(slot, dtype=jnp.int32)) < SEQ
    scale = 1.0 / math.sqrt(HEAD_DIM)

    def widen(rows):
        return jnp.pad(rows, ((0, padded - slot), (0, 0)))

    own_tokens = widen(tokens.reshape(slot, width))
    own_grad = cotangent.reshape(slot, width)
    own_grad = widen(jnp.where(own_live[:, None], own_grad, jnp.zeros_like(own_grad)))

    small = [ln1_gain, ln1_bias, b_qv[0], b_qv[1], b_out, ln2_gain, ln2_bias, b_down, b_up]
    sizes = [s.shape[0] for s in small]
    flat = sum(sizes)
    tile = 16 * LANES
    held = -(-flat // tile) * tile

    packed = jnp.pad(jnp.concatenate(small), (0, held - flat)).reshape(-1, LANES)
    all_tokens, qkv_full, out_full, all_small = exchange(
        "gather_first",
        0,
        [
            gather_tensor(own_tokens),
            gather_dp(w_qkv, 1),
            gather_dp(w_out, 1),
            gather_dp(packed, 0),
        ],
    )
    out_full = joined(out_full, 1)
    all_small = all_small.reshape(n_dp, held).astype(f32)
    pieces, start = [], 0
    for s in sizes:
        pieces.append(all_small[:, start : start + s].reshape(-1))
        start += s
    gain_one, shift_one, q_bias, v_bias, out_bias, gain_two, shift_two, down_bias, up_bias = pieces

    local_width = qkv_full.shape[2]
    heads_here = local_width // HEAD_DIM
    head_start = member * local_width
    q_own = lax.dynamic_slice_in_dim(q_bias, head_start, local_width, 0)
    v_own = lax.dynamic_slice_in_dim(v_bias, head_start, local_width, 0)

    def split_heads(values):
        return values.reshape(total, heads_here, HEAD_DIM)

    def scores_of(query_rows, key_rows):
        raw = (
            jnp.einsum(
                "qhe,khe->hqk",
                split_heads(query_rows),
                split_heads(key_rows),
                preferred_element_type=f32,
            )
            * scale
        )
        return jnp.where(key_live[None, None, :], raw, NEG)

    hat_one, _ = normalized(all_tokens.reshape(total, width).astype(f32))
    attn_rows = (hat_one * gain_one + shift_one).astype(bf16)
    projected = jnp.einsum("pd,cde->cpe", attn_rows, qkv_full, preferred_element_type=f32)
    queries = (projected[0] + q_own).astype(bf16)
    keys = projected[1].astype(bf16)
    values = (projected[2] + v_own).astype(bf16)
    scores = scores_of(queries, keys)
    top = jnp.max(scores, axis=-1, keepdims=True)
    expo = jnp.exp(scores - top)
    denom = jnp.sum(expo, axis=-1, keepdims=True)
    probs = expo / denom
    log_total = top + jnp.log(denom)
    mixed_heads = (
        jnp.einsum(
            "hqk,khe->qhe", probs.astype(bf16), split_heads(values), preferred_element_type=f32
        )
        .reshape(total, local_width)
        .astype(bf16)
    )
    branch_part = jnp.dot(mixed_heads, out_full, preferred_element_type=f32).astype(bf16)
    branch_parts, up_full, down_full = exchange(
        "sum_branch",
        1,
        [
            swap_tensor(branch_part.reshape(parts, padded, width)),
            gather_dp(w_up, 0),
            gather_dp(w_down, 1),
        ],
    )
    down_full = joined(down_full, 1)
    inputs = own_tokens.astype(f32)
    first = inputs + (summed(branch_parts) + out_bias)
    hidden_width = up_full.shape[1]
    hidden_start = member * hidden_width
    up_own = lax.dynamic_slice_in_dim(up_bias, hidden_start, hidden_width, 0)
    hat_two, scale_two = normalized(first)
    normed_two = (hat_two * gain_two + shift_two).astype(bf16)
    mlp_rows, grad_rows = exchange(
        "gather_second", 2, [gather_tensor(normed_two), gather_tensor(own_grad)]
    )
    mlp_rows = mlp_rows.reshape(total, width)
    grad_rows = grad_rows.reshape(total, width)
    pre_act = jnp.dot(mlp_rows, up_full, preferred_element_type=f32) + up_own
    activated = exact_gelu(pre_act).astype(bf16)
    down_part = jnp.dot(activated, down_full, preferred_element_type=f32).astype(bf16)
    grad_down = jnp.einsum("pf,pd->fd", activated, grad_rows, preferred_element_type=f32)
    grad_act = jnp.einsum("pd,fd->pf", grad_rows, down_full, preferred_element_type=f32)
    gelu_pull = jax.vjp(exact_gelu, pre_act)[1]
    grad_pre = gelu_pull(grad_act)[0].astype(bf16)
    grad_up = jnp.einsum("pd,pf->df", mlp_rows, grad_pre, preferred_element_type=f32)
    up_bias_grad = lax.dynamic_update_slice_in_dim(
        jnp.zeros(up_bias.shape, f32), jnp.sum(grad_pre.astype(f32), axis=0), hidden_start, 0
    )
    two_part = jnp.einsum("pf,df->pd", grad_pre, up_full, preferred_element_type=f32).astype(bf16)
    down_parts, two_parts, up_swapped, down_swapped = exchange(
        "sum_second",
        3,
        [
            swap_tensor(down_part.reshape(parts, padded, width)),
            swap_tensor(two_part.reshape(parts, padded, width)),
            swap_dp(grad_up.astype(bf16), 0),
            swap_dp(grad_down.astype(bf16), 1),
        ],
    )
    mixed = (first + summed(down_parts) + down_bias).astype(bf16)
    up_w_sum = summed(up_swapped)
    down_w_sum = summed(down_swapped)
    grad_normed_two = summed(two_parts)
    masked_float = own_grad.astype(f32)
    grad_first = masked_float + norm_back(grad_normed_two, gain_two, hat_two, scale_two)
    grad_gain_two = jnp.sum(grad_normed_two * hat_two, axis=0)
    grad_shift_two = jnp.sum(grad_normed_two, axis=0)
    grad_down_bias = jnp.sum(masked_float, axis=0)
    grad_branch = grad_first.astype(bf16)
    grad_out_bias = jnp.sum(grad_branch.astype(f32), axis=0)
    (branch_rows,) = exchange("gather_third", 4, [gather_tensor(grad_branch)])
    branch_rows = branch_rows.reshape(total, width)
    grad_out_w = jnp.einsum("pe,pd->ed", mixed_heads, branch_rows, preferred_element_type=f32)
    grad_heads = jnp.einsum("pd,ed->pe", branch_rows, out_full, preferred_element_type=f32).astype(
        bf16
    )
    grad_split = split_heads(grad_heads)
    probs_again = jnp.exp(scores_of(queries, keys) - log_total)
    grad_probs = jnp.einsum(
        "qhe,khe->hqk", grad_split, split_heads(values), preferred_element_type=f32
    )
    grad_values = (
        jnp.einsum("hqk,qhe->khe", probs_again.astype(bf16), grad_split, preferred_element_type=f32)
        .reshape(total, local_width)
        .astype(bf16)
    )
    inner = jnp.sum(probs_again * grad_probs, axis=-1, keepdims=True)
    grad_scores = (probs_again * (grad_probs - inner)).astype(bf16)
    grad_queries = (
        (
            jnp.einsum("hqk,khe->qhe", grad_scores, split_heads(keys), preferred_element_type=f32)
            * scale
        )
        .reshape(total, local_width)
        .astype(bf16)
    )
    grad_keys = (
        (
            jnp.einsum(
                "hqk,qhe->khe", grad_scores, split_heads(queries), preferred_element_type=f32
            )
            * scale
        )
        .reshape(total, local_width)
        .astype(bf16)
    )
    grad_qkv = jnp.stack([grad_queries, grad_keys, grad_values])
    grad_qkv_w = jnp.einsum("pd,cpe->cde", attn_rows, grad_qkv, preferred_element_type=f32)

    def own_columns(values):
        return lax.dynamic_update_slice_in_dim(
            jnp.zeros((local_width * parts,), f32),
            jnp.sum(values.astype(f32), axis=0),
            head_start,
            0,
        )

    one_part = jnp.einsum("cpe,cde->pd", grad_qkv, qkv_full, preferred_element_type=f32)
    grad_gain_one = jnp.sum(one_part * hat_one, axis=0)
    grad_shift_one = jnp.sum(one_part, axis=0)
    small_grads = [
        grad_gain_one,
        grad_shift_one,
        own_columns(grad_queries),
        own_columns(grad_values),
        grad_out_bias,
        grad_gain_two,
        grad_shift_two,
        grad_down_bias,
        up_bias_grad,
    ]
    packed_grads = jnp.concatenate([g.reshape(n_dp, -1) for g in small_grads], axis=1)
    packed_grads = jnp.pad(packed_grads, ((0, 0), (0, held - flat))).reshape(-1, LANES)
    one_parts, qkv_swapped, out_swapped, small_swapped = exchange(
        "sum_third",
        5,
        [
            swap_tensor(one_part.astype(bf16).reshape(parts, padded, width)),
            swap_dp(grad_qkv_w.astype(bf16), 1),
            swap_dp(grad_out_w.astype(bf16), 1),
            swap_dp(packed_grads, 0),
        ],
    )
    (small_all,) = exchange("sum_small", 6, [gather_tensor(summed(small_swapped))])
    hat_own, scale_own = normalized(inputs)
    grad_tokens = grad_first + norm_back(summed(one_parts), gain_one, hat_own, scale_own)
    small_sum = summed(small_all).reshape(held)
    done, start = [], 0
    for s in sizes:
        done.append(small_sum[start : start + s])
        start += s
    return (
        mixed[:slot].reshape(slot, images, width),
        grad_tokens[:slot].reshape(slot, images, width),
        done[0],
        done[1],
        summed(qkv_swapped),
        jnp.stack([done[2], done[3]]),
        summed(out_swapped),
        done[4],
        done[5],
        done[6],
        summed(up_swapped),
        done[8],
        down_w_sum,
        done[7],
    )


def solution(mesh):
    placed = (
        P("tensor", "dp", None),
        P("dp"),
        P("dp"),
        P(None, "dp", "tensor"),
        P(None, "dp"),
        P("tensor", "dp"),
        P("dp"),
        P("dp"),
        P("dp"),
        P("dp", "tensor"),
        P("dp"),
        P("tensor", "dp"),
        P("dp"),
        P("tensor", "dp", None),
    )
    return jax.shard_map(
        body,
        mesh=mesh,
        in_specs=placed,
        out_specs=(
            P("tensor", "dp", None),
            P("tensor", "dp", None),
            P("dp"),
            P("dp"),
            P(None, "dp", "tensor"),
            P(None, "dp"),
            P("tensor", "dp"),
            P("dp"),
            P("dp"),
            P("dp"),
            P("dp", "tensor"),
            P("dp"),
            P("tensor", "dp"),
            P("dp"),
        ),
        check_vma=False,
    )
```

```python
import math

import jax
import jax.numpy as jnp
from jax import lax
from jax.experimental import pallas as pl
from jax.experimental.pallas import tpu as pltpu
from jax.sharding import PartitionSpec as P

HEAD_DIM = 64
SEQ = 577
EPS = 1e-06
NEG = -1000000000.0
MESH = pl.DeviceIdType.MESH
LANES = 128


def at_dim(dim, size):
    def view(ref, j):
        start = pl.multiple_of(j * size, size)
        index = [slice(None)] * len(ref.shape)
        index[dim] = pl.ds(start, size)
        return ref.at[tuple(index)]

    return view


def at_front(ref, j):
    return ref.at[j]


def loop(first, last, step):
    def run(k, carry):
        step(k)
        return carry

    lax.fori_loop(first, last, run, 0)


class Item:
    def __init__(self, kind, array, out_shape, src, dst, turned=False):
        self.kind, self.array, self.src, self.dst = kind, array, src, dst
        self.turned = turned
        self.out = jax.ShapeDtypeStruct(out_shape, array.dtype)


def whole(ref, j):
    return ref


def gather_tensor(array, turned=False):
    n = lax.axis_size("tensor")
    return Item("tensor", array, (n, *array.shape), whole, at_front, turned)


def swap_tensor(array, turned=False):
    return Item("tensor", array, array.shape, at_front, at_front, turned)


def permuted(block, k):
    n = lax.axis_size("tensor")
    return lax.ppermute(block, "tensor", [(j, (j + k) % n) for j in range(n)])


def gather_dp(array, dim):
    n = lax.axis_size("dp")
    size = array.shape[dim]
    if dim == array.ndim - 1 and size % LANES:
        return Item("gather", array, (n, *array.shape), whole, at_front)
    shape = list(array.shape)
    shape[dim] *= n
    return Item("gather", array, tuple(shape), whole, at_dim(dim, size))


def joined(value, dim):
    if value.ndim == 2:
        return value
    moved = jnp.moveaxis(value, 0, dim)
    return moved.reshape(*moved.shape[:dim], -1, *moved.shape[dim + 2 :])


def swap_dp(array, dim):
    n = lax.axis_size("dp")
    size = array.shape[dim] // n
    shape = list(array.shape)
    shape[dim] = size
    if dim == array.ndim - 1 and size % LANES:
        parts = array.reshape(*array.shape[:dim], n, size)
        parts = jnp.moveaxis(parts, dim, 0)
        return Item("swap", parts, parts.shape, at_front, at_front)
    return Item("swap", array, (n, *shape), at_dim(dim, size), at_front)


def exchange(name, number, items, small=None):
    count = len(items)
    extra = 0 if small is None else 1
    n_t = lax.axis_size("tensor")
    n_dp = lax.axis_size("dp")
    chips = n_dp // 2
    with_tensor = any(i.kind == "tensor" for i in items)
    with_gather = any(i.kind == "gather" for i in items)
    with_swap = any(i.kind == "swap" for i in items)
    if extra:
        small_rows = small.shape[0] // n_dp

    def kernel(*refs):
        srcs = refs[:count]
        dsts = refs[count + extra : 2 * count + extra]
        scratch = refs[2 * (count + extra) :]
        own_sem, send, recv, fsend, frecv, ssend, srecv, tsend, trecv = scratch[:9]
        t = lax.axis_index("tensor")
        d = lax.axis_index("dp")
        core = lax.rem(d, 2)
        chip = d // 2
        sibling = d + 1 - 2 * core
        barrier = pltpu.get_barrier_semaphore()

        def hello(dp_id, t_id):
            pl.semaphore_signal(
                barrier, inc=1, device_id=(dp_id, t_id), device_id_type=MESH
            )

        def same_core(k):
            return lax.rem(chip + k, chips) * 2 + core

        greeted = 0
        if with_tensor:
            for k in range(1, n_t):
                hello(d, lax.rem(t + k, n_t))
            greeted += n_t - 1
        if with_swap:
            loop(1, n_dp, lambda k: hello(lax.rem(d + k, n_dp), t))
            greeted += n_dp - 1
        elif with_gather:
            loop(1, chips, lambda k: hello(same_core(k), t))
            hello(sibling, t)
            greeted += chips
        pl.semaphore_wait(barrier, greeted)

        def remote(src, dst, ssem, rsem, dp_id, t_id):
            return pltpu.make_async_remote_copy(
                src_ref=src,
                dst_ref=dst,
                send_sem=ssem,
                recv_sem=rsem,
                device_id=(dp_id, t_id),
                device_id_type=MESH,
            )

        def tensor_copy(i, k, owner):
            to = lax.rem(t + k, n_t)
            turned = items[i].turned
            return remote(
                items[i].src(srcs[i], (n_t - k) % n_t if turned else to),
                items[i].dst(dsts[i], k if turned else owner),
                tsend.at[i, k],
                trecv.at[i, k],
                d,
                to,
            )

        def swap_copy(i, k, owner):
            to = lax.rem(d + k, n_dp)
            return remote(
                items[i].src(srcs[i], to),
                items[i].dst(dsts[i], owner),
                ssend.at[i, k],
                srecv.at[i, k],
                to,
                t,
            )

        def gather_copy(i, k, owner):
            return remote(
                srcs[i],
                items[i].dst(dsts[i], owner),
                send.at[i, k],
                recv.at[i, k],
                same_core(k),
                t,
            )

        def forward_copy(i, k, owner, own):
            block = items[i].dst(dsts[i], owner)
            return remote(
                srcs[i] if own else block, block, fsend.at[i, k], frecv.at[i, k], sibling, t
            )

        def own_copy(i):
            me = t if items[i].kind == "tensor" else d
            me = 0 if items[i].turned else me
            return pltpu.make_async_copy(
                items[i].src(srcs[i], me), items[i].dst(dsts[i], me), own_sem.at[i]
            )

        if extra:
            small_in, small_out = refs[count], refs[2 * count + 1]
            small_got, small_sum, dsend, drecv, esend, erecv = scratch[9:]
            view = at_dim(0, small_rows)

            def small_swap(k, owner):
                to = lax.rem(d + k, n_dp)
                return remote(
                    view(small_in, to), small_got.at[owner], dsend.at[k], drecv.at[k], to, t
                )

            def small_gather(k, owner):
                to = lax.rem(t + k, n_t)
                return remote(
                    small_sum, small_out.at[owner], esend.at[k], erecv.at[k], d, to
                )

            loop(1, n_dp, lambda k: small_swap(k, d).start())

        def of(kind):
            return [i for i in range(count) if items[i].kind == kind]

        for k in (2, 3, 1) if n_t == 4 else range(1, n_t):
            for i in of("tensor"):
                tensor_copy(i, k, t).start()
        for i in of("gather"):
            loop(1, chips, lambda k, i=i: gather_copy(i, k, d).start())
            forward_copy(i, 0, d, True).start()
        for i in of("swap"):
            loop(1, n_dp, lambda k, i=i: swap_copy(i, k, d).start())
        for i in range(count):
            own_copy(i).start()
        if extra:
            small_got[d] = small_in[pl.ds(pl.multiple_of(d * small_rows, small_rows), small_rows)]
            loop(1, n_dp, lambda k: small_swap(k, lax.rem(d + n_dp - k, n_dp)).wait_recv())
            small_sum[...] = jnp.sum(small_got[...], axis=0)
            for k in range(1, n_t):
                small_gather(k, t).start()
            small_out[t] = small_sum[...]

        def came(k):
            return lax.rem(chip + chips - k, chips) * 2

        for i in of("gather"):

            def pass_on(k, i=i):
                gather_copy(i, k, came(k) + core).wait_recv()
                forward_copy(i, k, came(k) + core, False).start()

            loop(1, chips, pass_on)
        for i in of("gather"):
            other = 1 - core
            forward_copy(i, 0, came(0) + other, True).wait_recv()
            forward_copy(i, 0, d, True).wait_send()

            def finish(k, i=i):
                forward_copy(i, k, came(k) + other, False).wait_recv()
                forward_copy(i, k, came(k) + core, False).wait_send()
                gather_copy(i, k, d).wait_send()

            loop(1, chips, finish)
        for i in of("swap"):

            def end(k, i=i):
                swap_copy(i, k, lax.rem(d + n_dp - k, n_dp)).wait_recv()
                swap_copy(i, k, d).wait_send()

            loop(1, n_dp, end)
        for i in of("tensor"):
            for k in range(1, n_t):
                tensor_copy(i, k, lax.rem(t + n_t - k, n_t)).wait_recv()
                tensor_copy(i, k, t).wait_send()
        for i in range(count):
            own_copy(i).wait()
        if extra:
            loop(1, n_dp, lambda k: small_swap(k, d).wait_send())
            for k in range(1, n_t):
                small_gather(k, lax.rem(t + n_t - k, n_t)).wait_recv()
                small_gather(k, t).wait_send()

    dma = pltpu.SemaphoreType.DMA
    sent = sum(math.prod(i.out.shape) * i.out.dtype.itemsize for i in items)
    shapes = [i.out for i in items]
    specs = [pl.BlockSpec(memory_space=pl.ANY)] * count
    own_scratch = []
    arrays = [i.array for i in items]
    if extra:
        assert with_tensor and with_swap
        arrays.append(small)
        block = (small_rows, small.shape[1])
        shapes.append(jax.ShapeDtypeStruct((n_t, *block), small.dtype))
        specs.append(pl.BlockSpec(memory_space=pltpu.VMEM))
        own_scratch = [
            pltpu.VMEM((n_dp, *block), small.dtype),
            pltpu.VMEM(block, small.dtype),
            dma((n_dp,)),
            dma((n_dp,)),
            dma((n_t,)),
            dma((n_t,)),
        ]
    return pl.pallas_call(
        kernel,
        out_shape=tuple(shapes),
        in_specs=specs,
        out_specs=tuple(specs),
        scratch_shapes=[
            dma((count,)),
            dma((count, chips)),
            dma((count, chips)),
            dma((count, chips)),
            dma((count, chips)),
            dma((count, n_dp)),
            dma((count, n_dp)),
            dma((count, n_t)),
            dma((count, n_t)),
            *own_scratch,
        ],
        compiler_params=pltpu.CompilerParams(collective_id=number, has_side_effects=True),
        cost_estimate=pl.CostEstimate(flops=0, bytes_accessed=2 * sent, transcendentals=0),
        name=name,
    )(*arrays)


def side_by_side(pieces, sizes, held):
    placed, start = 0, 0
    for piece, size in zip(pieces, sizes):
        around = [(0, 0)] * (piece.ndim - 1) + [(start, held - start - size)]
        placed = placed + jnp.pad(piece, around)
        start += size
    return placed


def layer_norm(values, gain, shift):
    center = values - jnp.mean(values, axis=-1, keepdims=True)
    spread = jnp.mean(center * center, axis=-1, keepdims=True)
    return center * lax.rsqrt(spread + EPS) * gain + shift


def normalized(values):
    center = values - jnp.mean(values, axis=-1, keepdims=True)
    scale = lax.rsqrt(jnp.mean(center * center, axis=-1, keepdims=True) + EPS)
    return center * scale, scale


def norm_back(grad, gain, hat, scale):
    inner = grad * gain
    mean = jnp.mean(inner, axis=-1, keepdims=True)
    along = jnp.mean(inner * hat, axis=-1, keepdims=True)
    return (inner - mean - hat * along) * scale


def exact_gelu(values):
    return jax.nn.gelu(values, approximate=False)


def summed(parts):
    return jnp.sum(parts.astype(jnp.float32), axis=0)


def body(
    tokens,
    ln1_gain,
    ln1_bias,
    w_qkv,
    b_qv,
    w_out,
    b_out,
    ln2_gain,
    ln2_bias,
    w_up,
    b_up,
    w_down,
    b_down,
    cotangent,
):
    f32, bf16 = jnp.float32, jnp.bfloat16
    slot, images, width = tokens.shape
    parts = lax.axis_size("tensor")
    n_dp = lax.axis_size("dp")
    member = lax.axis_index("tensor")
    padded = -(-slot // 16) * 16
    total = padded * parts
    row = jnp.arange(padded, dtype=jnp.int32)
    at = (jnp.arange(parts, dtype=jnp.int32)[:, None] * slot + row[None, :]).reshape(total)
    key_live = (at < SEQ) & (jnp.tile(row, parts) < slot)
    own_live = (member * slot + jnp.arange(slot, dtype=jnp.int32)) < SEQ
    scale = 1.0 / math.sqrt(HEAD_DIM)

    def widen(rows):
        return jnp.pad(rows, ((0, padded - slot), (0, 0)))

    own_tokens = widen(tokens.reshape(slot, width))
    own_grad = cotangent.reshape(slot, width)
    own_grad = widen(jnp.where(own_live[:, None], own_grad, jnp.zeros_like(own_grad)))

    small = [ln1_gain, ln1_bias, b_qv[0], b_qv[1], b_out, ln2_gain, ln2_bias, b_down, b_up]
    sizes = [s.shape[0] for s in small]
    flat = sum(sizes)
    tile = 16 * LANES
    held = -(-flat // tile) * tile

    packed = side_by_side(small, sizes, held).reshape(-1, LANES)
    all_tokens, qkv_full, out_full, all_small = exchange(
        "gather_first",
        0,
        [
            gather_tensor(own_tokens),
            gather_dp(w_qkv, 1),
            gather_dp(w_out, 1),
            gather_dp(packed, 0),
        ],
    )
    out_full = joined(out_full, 1)
    all_tokens, own_grad = lax.optimization_barrier((all_tokens, own_grad))
    grad_blocks = [permuted(own_grad, k) for k in range(1, parts)]
    all_small = all_small.reshape(n_dp, held).astype(f32)
    pieces, start = [], 0
    for s in sizes:
        pieces.append(all_small[:, start : start + s].reshape(-1))
        start += s
    gain_one, shift_one, q_bias, v_bias, out_bias, gain_two, shift_two, down_bias, up_bias = pieces

    local_width = qkv_full.shape[2]
    heads_here = local_width // HEAD_DIM
    head_start = member * local_width
    q_own = lax.dynamic_slice_in_dim(q_bias, head_start, local_width, 0)
    v_own = lax.dynamic_slice_in_dim(v_bias, head_start, local_width, 0)

    def split_heads(values):
        return values.reshape(total, heads_here, HEAD_DIM)

    def scores_of(query_rows, key_rows):
        raw = (
            jnp.einsum(
                "qhe,khe->hqk",
                split_heads(query_rows),
                split_heads(key_rows),
                preferred_element_type=f32,
            )
            * scale
        )
        return jnp.where(key_live[None, None, :], raw, NEG)

    hat_one, _ = normalized(all_tokens.reshape(total, width).astype(f32))
    attn_rows = (hat_one * gain_one + shift_one).astype(bf16)
    projected = jnp.einsum("pd,cde->cpe", attn_rows, qkv_full, preferred_element_type=f32)
    queries = (projected[0] + q_own).astype(bf16)
    keys = projected[1].astype(bf16)
    values = (projected[2] + v_own).astype(bf16)
    scores = scores_of(queries, keys)
    top = jnp.max(scores, axis=-1, keepdims=True)
    expo = jnp.exp(scores - top)
    denom = jnp.sum(expo, axis=-1, keepdims=True)
    probs = expo / denom
    log_total = top + jnp.log(denom)
    mixed_heads = (
        jnp.einsum(
            "hqk,khe->qhe", probs.astype(bf16), split_heads(values), preferred_element_type=f32
        )
        .reshape(total, local_width)
        .astype(bf16)
    )
    branch_part = jnp.dot(mixed_heads, out_full, preferred_element_type=f32).astype(bf16)
    branch_part, grad_blocks = lax.optimization_barrier((branch_part, grad_blocks))
    grad_rows = jnp.concatenate([own_grad, *grad_blocks])
    branch_parts, up_full, down_full = exchange(
        "sum_branch",
        1,
        [
            swap_tensor(branch_part.reshape(parts, padded, width)),
            gather_dp(w_up, 0),
            gather_dp(w_down, 1),
        ],
    )
    down_full = joined(down_full, 1)
    inputs = own_tokens.astype(f32)
    first = inputs + (summed(branch_parts) + out_bias)
    hidden_width = up_full.shape[1]
    hidden_start = member * hidden_width
    up_own = lax.dynamic_slice_in_dim(up_bias, hidden_start, hidden_width, 0)
    hat_two, scale_two = normalized(first)
    normed_two = (hat_two * gain_two + shift_two).astype(bf16)
    (mlp_rows,) = exchange("gather_second", 2, [gather_tensor(normed_two, turned=True)])
    mlp_rows = mlp_rows.reshape(total, width)
    pre_act = jnp.dot(mlp_rows, up_full, preferred_element_type=f32) + up_own
    activated = exact_gelu(pre_act).astype(bf16)
    down_part = jnp.dot(activated, down_full, preferred_element_type=f32).astype(bf16)
    grad_down = jnp.einsum("pf,pd->fd", activated, grad_rows, preferred_element_type=f32)
    grad_act = jnp.einsum("pd,fd->pf", grad_rows, down_full, preferred_element_type=f32)
    gelu_pull = jax.vjp(exact_gelu, pre_act)[1]
    grad_pre = gelu_pull(grad_act)[0].astype(bf16)
    grad_up = jnp.einsum("pd,pf->df", mlp_rows, grad_pre, preferred_element_type=f32)
    up_bias_grad = lax.dynamic_update_slice_in_dim(
        jnp.zeros(up_bias.shape, f32), jnp.sum(grad_pre.astype(f32), axis=0), hidden_start, 0
    )
    two_part = jnp.einsum("pf,df->pd", grad_pre, up_full, preferred_element_type=f32).astype(bf16)
    two_parts, up_swapped = exchange(
        "sum_second",
        3,
        [
            swap_tensor(two_part.reshape(parts, padded, width), turned=True),
            swap_dp(grad_up.astype(bf16), 0),
        ],
    )
    grad_normed_two = summed(two_parts)
    masked_float = own_grad.astype(f32)
    grad_first = masked_float + norm_back(grad_normed_two, gain_two, hat_two, scale_two)
    grad_gain_two = jnp.sum(grad_normed_two * hat_two, axis=0)
    grad_shift_two = jnp.sum(grad_normed_two, axis=0)
    grad_down_bias = jnp.sum(masked_float, axis=0)
    grad_branch = grad_first.astype(bf16)
    grad_out_bias = jnp.sum(grad_branch.astype(f32), axis=0)
    branch_rows, down_swapped = exchange(
        "gather_third", 4, [gather_tensor(grad_branch), swap_dp(grad_down.astype(bf16), 1)]
    )
    branch_rows, down_part = lax.optimization_barrier((branch_rows, down_part))
    down_blocks = down_part.reshape(parts, padded, width)
    down_parts = [permuted(down_blocks[parts - k], k) for k in (1, parts - 1)]
    branch_rows = branch_rows.reshape(total, width)
    grad_out_w = jnp.einsum("pe,pd->ed", mixed_heads, branch_rows, preferred_element_type=f32)
    grad_heads = jnp.einsum("pd,ed->pe", branch_rows, out_full, preferred_element_type=f32).astype(
        bf16
    )
    grad_split = split_heads(grad_heads)
    probs_again = jnp.exp(scores_of(queries, keys) - log_total)
    grad_probs = jnp.einsum(
        "qhe,khe->hqk", grad_split, split_heads(values), preferred_element_type=f32
    )
    grad_values = (
        jnp.einsum("hqk,qhe->khe", probs_again.astype(bf16), grad_split, preferred_element_type=f32)
        .reshape(total, local_width)
        .astype(bf16)
    )
    inner = jnp.sum(probs_again * grad_probs, axis=-1, keepdims=True)
    inner, down_parts, down_blocks = lax.optimization_barrier((inner, down_parts, down_blocks))
    down_parts += [permuted(down_blocks[parts - k], k) for k in range(2, parts - 1)]
    grad_scores = (probs_again * (grad_probs - inner)).astype(bf16)
    grad_queries = (
        (
            jnp.einsum("hqk,khe->qhe", grad_scores, split_heads(keys), preferred_element_type=f32)
            * scale
        )
        .reshape(total, local_width)
        .astype(bf16)
    )
    grad_keys = (
        (
            jnp.einsum(
                "hqk,qhe->khe", grad_scores, split_heads(queries), preferred_element_type=f32
            )
            * scale
        )
        .reshape(total, local_width)
        .astype(bf16)
    )
    grad_qkv = jnp.stack([grad_queries, grad_keys, grad_values])
    grad_qkv_w = jnp.einsum("pd,cpe->cde", attn_rows, grad_qkv, preferred_element_type=f32)

    def own_columns(values):
        return lax.dynamic_update_slice_in_dim(
            jnp.zeros((local_width * parts,), f32),
            jnp.sum(values.astype(f32), axis=0),
            head_start,
            0,
        )

    one_part = jnp.einsum("cpe,cde->pd", grad_qkv, qkv_full, preferred_element_type=f32)
    grad_gain_one = jnp.sum(one_part * hat_one, axis=0)
    grad_shift_one = jnp.sum(one_part, axis=0)
    small_grads = [
        grad_gain_one,
        grad_shift_one,
        own_columns(grad_queries),
        own_columns(grad_values),
        grad_out_bias,
        grad_gain_two,
        grad_shift_two,
        grad_down_bias,
        up_bias_grad,
    ]
    packed_grads = side_by_side([g.reshape(n_dp, -1) for g in small_grads], sizes, held)
    packed_grads = packed_grads.reshape(-1, LANES)
    one_part, down_parts = lax.optimization_barrier((one_part.astype(bf16), down_parts))
    down_sum = down_blocks[0].astype(f32)
    for part in down_parts:
        down_sum = down_sum + part.astype(f32)
    mixed = (first + down_sum + down_bias).astype(bf16)
    one_parts, qkv_swapped, out_swapped, small_all = exchange(
        "sum_third",
        5,
        [
            swap_tensor(one_part.reshape(parts, padded, width)),
            swap_dp(grad_qkv_w.astype(bf16), 1),
            swap_dp(grad_out_w.astype(bf16), 1),
        ],
        packed_grads,
    )
    hat_own, scale_own = normalized(inputs)
    grad_tokens = grad_first + norm_back(summed(one_parts), gain_one, hat_own, scale_own)
    small_sum = summed(small_all).reshape(held)
    done, start = [], 0
    for s in sizes:
        done.append(small_sum[start : start + s])
        start += s
    return (
        mixed[:slot].reshape(slot, images, width),
        grad_tokens[:slot].reshape(slot, images, width),
        done[0],
        done[1],
        summed(qkv_swapped),
        jnp.stack([done[2], done[3]]),
        summed(out_swapped),
        done[4],
        done[5],
        done[6],
        summed(up_swapped),
        done[8],
        summed(down_swapped),
        done[7],
    )


def solution(mesh):
    placed = (
        P("tensor", "dp", None),
        P("dp"),
        P("dp"),
        P(None, "dp", "tensor"),
        P(None, "dp"),
        P("tensor", "dp"),
        P("dp"),
        P("dp"),
        P("dp"),
        P("dp", "tensor"),
        P("dp"),
        P("tensor", "dp"),
        P("dp"),
        P("tensor", "dp", None),
    )
    return jax.shard_map(
        body,
        mesh=mesh,
        in_specs=placed,
        out_specs=(
            P("tensor", "dp", None),
            P("tensor", "dp", None),
            P("dp"),
            P("dp"),
            P(None, "dp", "tensor"),
            P(None, "dp"),
            P("tensor", "dp"),
            P("dp"),
            P("dp"),
            P("dp"),
            P("dp", "tensor"),
            P("dp"),
            P("tensor", "dp"),
            P("dp"),
        ),
        check_vma=False,
    )
```

```python
import math

import jax
import jax.numpy as jnp
from jax import lax
from jax.experimental import pallas as pl
from jax.experimental.pallas import tpu as pltpu
from jax.sharding import PartitionSpec as P

HEAD_DIM = 64
SEQ = 577
EPS = 1e-06
NEG = -1000000000.0
MESH = pl.DeviceIdType.MESH
LANES = 128


def at_dim(dim, size):
    def view(ref, j):
        start = pl.multiple_of(j * size, size)
        index = [slice(None)] * len(ref.shape)
        index[dim] = pl.ds(start, size)
        return ref.at[tuple(index)]

    return view


def at_front(ref, j):
    return ref.at[j]


def loop(first, last, step):
    def run(k, carry):
        step(k)
        return carry

    lax.fori_loop(first, last, run, 0)


class Item:
    def __init__(self, kind, array, out_shape, src, dst, turned=False):
        self.kind, self.array, self.src, self.dst = kind, array, src, dst
        self.turned = turned
        self.out = jax.ShapeDtypeStruct(out_shape, array.dtype)


def whole(ref, j):
    return ref


def gather_tensor(array, turned=False):
    n = lax.axis_size("tensor")
    return Item("tensor", array, (n, *array.shape), whole, at_front, turned)


def swap_tensor(array, turned=False):
    return Item("tensor", array, array.shape, at_front, at_front, turned)


def permuted(block, k):
    n = lax.axis_size("tensor")
    return lax.ppermute(block, "tensor", [(j, (j + k) % n) for j in range(n)])


def gather_dp(array, dim):
    n = lax.axis_size("dp")
    size = array.shape[dim]
    if dim == array.ndim - 1 and size % LANES:
        return Item("gather", array, (n, *array.shape), whole, at_front)
    shape = list(array.shape)
    shape[dim] *= n
    return Item("gather", array, tuple(shape), whole, at_dim(dim, size))


def joined(value, dim):
    if value.ndim == 2:
        return value
    moved = jnp.moveaxis(value, 0, dim)
    return moved.reshape(*moved.shape[:dim], -1, *moved.shape[dim + 2 :])


def swap_dp(array, dim):
    n = lax.axis_size("dp")
    size = array.shape[dim] // n
    shape = list(array.shape)
    shape[dim] = size
    if dim == array.ndim - 1 and size % LANES:
        parts = array.reshape(*array.shape[:dim], n, size)
        parts = jnp.moveaxis(parts, dim, 0)
        return Item("swap", parts, parts.shape, at_front, at_front)
    return Item("swap", array, (n, *shape), at_dim(dim, size), at_front)


def exchange(name, number, items, small=None):
    count = len(items)
    extra = 0 if small is None else 1
    n_t = lax.axis_size("tensor")
    n_dp = lax.axis_size("dp")
    chips = n_dp // 2
    with_tensor = any(i.kind == "tensor" for i in items)
    with_gather = any(i.kind == "gather" for i in items)
    with_swap = any(i.kind == "swap" for i in items)
    if extra:
        small_rows = small.shape[0] // n_dp

    def kernel(*refs):
        srcs = refs[:count]
        dsts = refs[count + extra : 2 * count + extra]
        scratch = refs[2 * (count + extra) :]
        own_sem, send, recv, fsend, frecv, ssend, srecv, tsend, trecv, rsend = scratch[:10]
        t = lax.axis_index("tensor")
        d = lax.axis_index("dp")
        core = lax.rem(d, 2)
        chip = d // 2
        sibling = d + 1 - 2 * core
        barrier = pltpu.get_barrier_semaphore()

        def hello(dp_id, t_id):
            pl.semaphore_signal(
                barrier, inc=1, device_id=(dp_id, t_id), device_id_type=MESH
            )

        def same_core(k):
            return lax.rem(chip + k, chips) * 2 + core

        greeted = 0
        if with_tensor:
            for k in range(1, n_t):
                hello(d, lax.rem(t + k, n_t))
            greeted += n_t - 1
        if with_swap:
            loop(1, n_dp, lambda k: hello(lax.rem(d + k, n_dp), t))
            greeted += n_dp - 1
        elif with_gather:
            loop(1, chips, lambda k: hello(same_core(k), t))
            hello(sibling, t)
            greeted += chips
        pl.semaphore_wait(barrier, greeted)

        def remote(src, dst, ssem, rsem, dp_id, t_id):
            return pltpu.make_async_remote_copy(
                src_ref=src,
                dst_ref=dst,
                send_sem=ssem,
                recv_sem=rsem,
                device_id=(dp_id, t_id),
                device_id_type=MESH,
            )

        def tensor_copy(i, k, owner):
            to = lax.rem(t + k, n_t)
            turned = items[i].turned
            return remote(
                items[i].src(srcs[i], (n_t - k) % n_t if turned else to),
                items[i].dst(dsts[i], k if turned else owner),
                tsend.at[i, k],
                trecv.at[i, k],
                d,
                to,
            )

        def swap_copy(i, k, owner):
            to = lax.rem(d + k, n_dp)
            return remote(
                items[i].src(srcs[i], to),
                items[i].dst(dsts[i], owner),
                ssend.at[i, k],
                srecv.at[i, k],
                to,
                t,
            )

        def gather_copy(i, k, owner):
            return remote(
                srcs[i],
                items[i].dst(dsts[i], owner),
                send.at[i, k],
                recv.at[i, k],
                same_core(k),
                t,
            )

        def forward_copy(i, k, owner, own):
            block = items[i].dst(dsts[i], owner)
            return remote(
                srcs[i] if own else block, block, fsend.at[i, k], frecv.at[i, k], sibling, t
            )

        def own_copy(i):
            me = t if items[i].kind == "tensor" else d
            me = 0 if items[i].turned else me
            return pltpu.make_async_copy(
                items[i].src(srcs[i], me), items[i].dst(dsts[i], me), own_sem.at[i]
            )

        if extra:
            small_in, small_out = refs[count], refs[2 * count + 1]
            small_got, small_sum, dsend, drecv, esend, erecv = scratch[10:]
            view = at_dim(0, small_rows)

            def small_swap(k, owner):
                to = lax.rem(d + k, n_dp)
                return remote(
                    view(small_in, to), small_got.at[owner], dsend.at[k], drecv.at[k], to, t
                )

            def small_gather(k, owner):
                to = lax.rem(t + k, n_t)
                return remote(
                    small_sum, small_out.at[owner], esend.at[k], erecv.at[k], d, to
                )

            loop(1, n_dp, lambda k: small_swap(k, d).start())

        def of(kind):
            return [i for i in range(count) if items[i].kind == kind]

        def relayed(i):
            return n_t == 4 and items[i].src is whole

        def relay_copy(i):
            block = items[i].dst(dsts[i], 2 if items[i].turned else (2 - t) * 3)
            landing = items[i].dst(dsts[i], 2 * t - 1 if items[i].turned else (2 - t) * 3)
            k = 2 * t - 1
            return remote(block, landing, rsend.at[i], trecv.at[i, k], d, (t - 1) * 3)

        def unless_relayed(i, k, act):
            if relayed(i) and k != 2:
                pl.when(t != (0 if k == 3 else 3))(act)
            else:
                act()

        for k in (2, 3, 1) if n_t == 4 else range(1, n_t):
            for i in of("tensor"):
                unless_relayed(i, k, lambda i=i, k=k: tensor_copy(i, k, t).start())
        for i in of("gather"):
            loop(1, chips, lambda k, i=i: gather_copy(i, k, d).start())
            forward_copy(i, 0, d, True).start()
        for i in of("swap"):
            loop(1, n_dp, lambda k, i=i: swap_copy(i, k, d).start())
        for i in range(count):
            own_copy(i).start()
        if extra:
            small_got[d] = small_in[pl.ds(pl.multiple_of(d * small_rows, small_rows), small_rows)]
            loop(1, n_dp, lambda k: small_swap(k, lax.rem(d + n_dp - k, n_dp)).wait_recv())
            small_sum[...] = jnp.sum(small_got[...], axis=0)
            for k in range(1, n_t):
                small_gather(k, t).start()
            small_out[t] = small_sum[...]

        middle = (t == 1) | (t == 2)

        def relay_all():
            for i in of("tensor"):
                if relayed(i):
                    tensor_copy(i, 2, lax.rem(t + n_t - 2, n_t)).wait_recv()

                    @pl.when(middle)
                    def _(i=i):
                        relay_copy(i).start()

        if not with_gather:
            relay_all()

        def came(k):
            return lax.rem(chip + chips - k, chips) * 2

        for i in of("gather"):

            def pass_on(k, i=i):
                gather_copy(i, k, came(k) + core).wait_recv()
                forward_copy(i, k, came(k) + core, False).start()

            loop(1, chips, pass_on)
        if with_gather:
            relay_all()
        for i in of("gather"):
            other = 1 - core
            forward_copy(i, 0, came(0) + other, True).wait_recv()
            forward_copy(i, 0, d, True).wait_send()

            def finish(k, i=i):
                forward_copy(i, k, came(k) + other, False).wait_recv()
                forward_copy(i, k, came(k) + core, False).wait_send()
                gather_copy(i, k, d).wait_send()

            loop(1, chips, finish)
        for i in of("swap"):

            def end(k, i=i):
                swap_copy(i, k, lax.rem(d + n_dp - k, n_dp)).wait_recv()
                swap_copy(i, k, d).wait_send()

            loop(1, n_dp, end)
        for i in of("tensor"):
            for k in range(1, n_t):
                if not (relayed(i) and k == 2):
                    tensor_copy(i, k, lax.rem(t + n_t - k, n_t)).wait_recv()
                unless_relayed(i, k, lambda i=i, k=k: tensor_copy(i, k, t).wait_send())
            if relayed(i):

                @pl.when(middle)
                def _(i=i):
                    relay_copy(i).wait_send()

        for i in range(count):
            own_copy(i).wait()
        if extra:
            loop(1, n_dp, lambda k: small_swap(k, d).wait_send())
            for k in range(1, n_t):
                small_gather(k, lax.rem(t + n_t - k, n_t)).wait_recv()
                small_gather(k, t).wait_send()

    dma = pltpu.SemaphoreType.DMA
    sent = sum(math.prod(i.out.shape) * i.out.dtype.itemsize for i in items)
    shapes = [i.out for i in items]
    specs = [pl.BlockSpec(memory_space=pl.ANY)] * count
    own_scratch = []
    arrays = [i.array for i in items]
    if extra:
        assert with_tensor and with_swap
        arrays.append(small)
        block = (small_rows, small.shape[1])
        shapes.append(jax.ShapeDtypeStruct((n_t, *block), small.dtype))
        specs.append(pl.BlockSpec(memory_space=pltpu.VMEM))
        own_scratch = [
            pltpu.VMEM((n_dp, *block), small.dtype),
            pltpu.VMEM(block, small.dtype),
            dma((n_dp,)),
            dma((n_dp,)),
            dma((n_t,)),
            dma((n_t,)),
        ]
    return pl.pallas_call(
        kernel,
        out_shape=tuple(shapes),
        in_specs=specs,
        out_specs=tuple(specs),
        scratch_shapes=[
            dma((count,)),
            dma((count, chips)),
            dma((count, chips)),
            dma((count, chips)),
            dma((count, chips)),
            dma((count, n_dp)),
            dma((count, n_dp)),
            dma((count, n_t)),
            dma((count, n_t)),
            dma((count,)),
            *own_scratch,
        ],
        compiler_params=pltpu.CompilerParams(collective_id=number, has_side_effects=True),
        cost_estimate=pl.CostEstimate(flops=0, bytes_accessed=2 * sent, transcendentals=0),
        name=name,
    )(*arrays)


def side_by_side(pieces, sizes, held):
    placed, start = 0, 0
    for piece, size in zip(pieces, sizes):
        around = [(0, 0)] * (piece.ndim - 1) + [(start, held - start - size)]
        placed = placed + jnp.pad(piece, around)
        start += size
    return placed


def layer_norm(values, gain, shift):
    center = values - jnp.mean(values, axis=-1, keepdims=True)
    spread = jnp.mean(center * center, axis=-1, keepdims=True)
    return center * lax.rsqrt(spread + EPS) * gain + shift


def normalized(values):
    center = values - jnp.mean(values, axis=-1, keepdims=True)
    scale = lax.rsqrt(jnp.mean(center * center, axis=-1, keepdims=True) + EPS)
    return center * scale, scale


def norm_back(grad, gain, hat, scale):
    inner = grad * gain
    mean = jnp.mean(inner, axis=-1, keepdims=True)
    along = jnp.mean(inner * hat, axis=-1, keepdims=True)
    return (inner - mean - hat * along) * scale


def exact_gelu(values):
    return jax.nn.gelu(values, approximate=False)


def summed(parts):
    return jnp.sum(parts.astype(jnp.float32), axis=0)


def body(
    tokens,
    ln1_gain,
    ln1_bias,
    w_qkv,
    b_qv,
    w_out,
    b_out,
    ln2_gain,
    ln2_bias,
    w_up,
    b_up,
    w_down,
    b_down,
    cotangent,
):
    f32, bf16 = jnp.float32, jnp.bfloat16
    slot, images, width = tokens.shape
    parts = lax.axis_size("tensor")
    n_dp = lax.axis_size("dp")
    member = lax.axis_index("tensor")
    padded = -(-slot // 16) * 16
    total = padded * parts
    row = jnp.arange(padded, dtype=jnp.int32)
    at = (jnp.arange(parts, dtype=jnp.int32)[:, None] * slot + row[None, :]).reshape(total)
    key_live = (at < SEQ) & (jnp.tile(row, parts) < slot)
    own_live = (member * slot + jnp.arange(slot, dtype=jnp.int32)) < SEQ
    scale = 1.0 / math.sqrt(HEAD_DIM)

    def widen(rows):
        return jnp.pad(rows, ((0, padded - slot), (0, 0)))

    own_tokens = widen(tokens.reshape(slot, width))
    own_grad = cotangent.reshape(slot, width)
    own_grad = widen(jnp.where(own_live[:, None], own_grad, jnp.zeros_like(own_grad)))

    small = [ln1_gain, ln1_bias, b_qv[0], b_qv[1], b_out, ln2_gain, ln2_bias, b_down, b_up]
    sizes = [s.shape[0] for s in small]
    flat = sum(sizes)
    tile = 16 * LANES
    held = -(-flat // tile) * tile

    packed = side_by_side(small, sizes, held).reshape(-1, LANES)
    all_tokens, qkv_full, out_full, all_small = exchange(
        "gather_first",
        0,
        [
            gather_tensor(own_tokens),
            gather_dp(w_qkv, 1),
            gather_dp(w_out, 1),
            gather_dp(packed, 0),
        ],
    )
    out_full = joined(out_full, 1)
    all_tokens, own_grad = lax.optimization_barrier((all_tokens, own_grad))
    grad_blocks = [permuted(own_grad, k) for k in range(1, parts)]
    all_small = all_small.reshape(n_dp, held).astype(f32)
    pieces, start = [], 0
    for s in sizes:
        pieces.append(all_small[:, start : start + s].reshape(-1))
        start += s
    gain_one, shift_one, q_bias, v_bias, out_bias, gain_two, shift_two, down_bias, up_bias = pieces

    local_width = qkv_full.shape[2]
    heads_here = local_width // HEAD_DIM
    head_start = member * local_width
    q_own = lax.dynamic_slice_in_dim(q_bias, head_start, local_width, 0)
    v_own = lax.dynamic_slice_in_dim(v_bias, head_start, local_width, 0)

    def split_heads(values):
        return values.reshape(total, heads_here, HEAD_DIM)

    def scores_of(query_rows, key_rows):
        raw = (
            jnp.einsum(
                "qhe,khe->hqk",
                split_heads(query_rows),
                split_heads(key_rows),
                preferred_element_type=f32,
            )
            * scale
        )
        return jnp.where(key_live[None, None, :], raw, NEG)

    hat_one, _ = normalized(all_tokens.reshape(total, width).astype(f32))
    attn_rows = (hat_one * gain_one + shift_one).astype(bf16)
    projected = jnp.einsum("pd,cde->cpe", attn_rows, qkv_full, preferred_element_type=f32)
    queries = (projected[0] + q_own).astype(bf16)
    keys = projected[1].astype(bf16)
    values = (projected[2] + v_own).astype(bf16)
    scores = scores_of(queries, keys)
    top = jnp.max(scores, axis=-1, keepdims=True)
    expo = jnp.exp(scores - top)
    denom = jnp.sum(expo, axis=-1, keepdims=True)
    probs = expo / denom
    log_total = top + jnp.log(denom)
    mixed_heads = (
        jnp.einsum(
            "hqk,khe->qhe", probs.astype(bf16), split_heads(values), preferred_element_type=f32
        )
        .reshape(total, local_width)
        .astype(bf16)
    )
    branch_part = jnp.dot(mixed_heads, out_full, preferred_element_type=f32).astype(bf16)
    branch_part, grad_blocks = lax.optimization_barrier((branch_part, grad_blocks))
    grad_rows = jnp.concatenate([own_grad, *grad_blocks])
    branch_parts, up_full, down_full = exchange(
        "sum_branch",
        1,
        [
            swap_tensor(branch_part.reshape(parts, padded, width)),
            gather_dp(w_up, 0),
            gather_dp(w_down, 1),
        ],
    )
    down_full = joined(down_full, 1)
    inputs = own_tokens.astype(f32)
    first = inputs + (summed(branch_parts) + out_bias)
    hidden_width = up_full.shape[1]
    hidden_start = member * hidden_width
    up_own = lax.dynamic_slice_in_dim(up_bias, hidden_start, hidden_width, 0)
    hat_two, scale_two = normalized(first)
    normed_two = (hat_two * gain_two + shift_two).astype(bf16)
    (mlp_rows,) = exchange("gather_second", 2, [gather_tensor(normed_two, turned=True)])
    mlp_rows = mlp_rows.reshape(total, width)
    pre_act = jnp.dot(mlp_rows, up_full, preferred_element_type=f32) + up_own
    activated = exact_gelu(pre_act).astype(bf16)
    down_part = jnp.dot(activated, down_full, preferred_element_type=f32).astype(bf16)
    grad_down = jnp.einsum("pf,pd->fd", activated, grad_rows, preferred_element_type=f32)
    grad_act = jnp.einsum("pd,fd->pf", grad_rows, down_full, preferred_element_type=f32)
    gelu_pull = jax.vjp(exact_gelu, pre_act)[1]
    grad_pre = gelu_pull(grad_act)[0].astype(bf16)
    grad_up = jnp.einsum("pd,pf->df", mlp_rows, grad_pre, preferred_element_type=f32)
    up_bias_grad = lax.dynamic_update_slice_in_dim(
        jnp.zeros(up_bias.shape, f32), jnp.sum(grad_pre.astype(f32), axis=0), hidden_start, 0
    )
    two_part = jnp.einsum("pf,df->pd", grad_pre, up_full, preferred_element_type=f32).astype(bf16)
    two_parts, up_swapped = exchange(
        "sum_second",
        3,
        [
            swap_tensor(two_part.reshape(parts, padded, width), turned=True),
            swap_dp(grad_up.astype(bf16), 0),
        ],
    )
    grad_normed_two = summed(two_parts)
    masked_float = own_grad.astype(f32)
    grad_first = masked_float + norm_back(grad_normed_two, gain_two, hat_two, scale_two)
    grad_gain_two = jnp.sum(grad_normed_two * hat_two, axis=0)
    grad_shift_two = jnp.sum(grad_normed_two, axis=0)
    grad_down_bias = jnp.sum(masked_float, axis=0)
    grad_branch = grad_first.astype(bf16)
    grad_out_bias = jnp.sum(grad_branch.astype(f32), axis=0)
    branch_rows, down_swapped = exchange(
        "gather_third", 4, [gather_tensor(grad_branch), swap_dp(grad_down.astype(bf16), 1)]
    )
    branch_rows, down_part = lax.optimization_barrier((branch_rows, down_part))
    down_blocks = down_part.reshape(parts, padded, width)
    down_parts = [permuted(down_blocks[parts - k], k) for k in (1, parts - 1)]
    branch_rows = branch_rows.reshape(total, width)
    grad_out_w = jnp.einsum("pe,pd->ed", mixed_heads, branch_rows, preferred_element_type=f32)
    grad_heads = jnp.einsum("pd,ed->pe", branch_rows, out_full, preferred_element_type=f32).astype(
        bf16
    )
    grad_split = split_heads(grad_heads)
    probs_again = jnp.exp(scores_of(queries, keys) - log_total)
    grad_probs = jnp.einsum(
        "qhe,khe->hqk", grad_split, split_heads(values), preferred_element_type=f32
    )
    grad_values = (
        jnp.einsum("hqk,qhe->khe", probs_again.astype(bf16), grad_split, preferred_element_type=f32)
        .reshape(total, local_width)
        .astype(bf16)
    )
    inner = jnp.sum(probs_again * grad_probs, axis=-1, keepdims=True)
    inner, down_parts, down_blocks = lax.optimization_barrier((inner, down_parts, down_blocks))
    down_parts += [permuted(down_blocks[parts - k], k) for k in range(2, parts - 1)]
    grad_scores = (probs_again * (grad_probs - inner)).astype(bf16)
    grad_queries = (
        (
            jnp.einsum("hqk,khe->qhe", grad_scores, split_heads(keys), preferred_element_type=f32)
            * scale
        )
        .reshape(total, local_width)
        .astype(bf16)
    )
    grad_keys = (
        (
            jnp.einsum(
                "hqk,qhe->khe", grad_scores, split_heads(queries), preferred_element_type=f32
            )
            * scale
        )
        .reshape(total, local_width)
        .astype(bf16)
    )
    grad_qkv = jnp.stack([grad_queries, grad_keys, grad_values])
    grad_qkv_w = jnp.einsum("pd,cpe->cde", attn_rows, grad_qkv, preferred_element_type=f32)

    def own_columns(values):
        return lax.dynamic_update_slice_in_dim(
            jnp.zeros((local_width * parts,), f32),
            jnp.sum(values.astype(f32), axis=0),
            head_start,
            0,
        )

    one_part = jnp.einsum("cpe,cde->pd", grad_qkv, qkv_full, preferred_element_type=f32)
    grad_gain_one = jnp.sum(one_part * hat_one, axis=0)
    grad_shift_one = jnp.sum(one_part, axis=0)
    small_grads = [
        grad_gain_one,
        grad_shift_one,
        own_columns(grad_queries),
        own_columns(grad_values),
        grad_out_bias,
        grad_gain_two,
        grad_shift_two,
        grad_down_bias,
        up_bias_grad,
    ]
    packed_grads = side_by_side([g.reshape(n_dp, -1) for g in small_grads], sizes, held)
    packed_grads = packed_grads.reshape(-1, LANES)
    one_part, down_parts = lax.optimization_barrier((one_part.astype(bf16), down_parts))
    down_sum = down_blocks[0].astype(f32)
    for part in down_parts:
        down_sum = down_sum + part.astype(f32)
    mixed = (first + down_sum + down_bias).astype(bf16)
    one_parts, qkv_swapped, out_swapped, small_all = exchange(
        "sum_third",
        5,
        [
            swap_tensor(one_part.reshape(parts, padded, width)),
            swap_dp(grad_qkv_w.astype(bf16), 1),
            swap_dp(grad_out_w.astype(bf16), 1),
        ],
        packed_grads,
    )
    hat_own, scale_own = normalized(inputs)
    grad_tokens = grad_first + norm_back(summed(one_parts), gain_one, hat_own, scale_own)
    small_sum = summed(small_all).reshape(held)
    done, start = [], 0
    for s in sizes:
        done.append(small_sum[start : start + s])
        start += s
    return (
        mixed[:slot].reshape(slot, images, width),
        grad_tokens[:slot].reshape(slot, images, width),
        done[0],
        done[1],
        summed(qkv_swapped),
        jnp.stack([done[2], done[3]]),
        summed(out_swapped),
        done[4],
        done[5],
        done[6],
        summed(up_swapped),
        done[8],
        summed(down_swapped),
        done[7],
    )


def solution(mesh):
    placed = (
        P("tensor", "dp", None),
        P("dp"),
        P("dp"),
        P(None, "dp", "tensor"),
        P(None, "dp"),
        P("tensor", "dp"),
        P("dp"),
        P("dp"),
        P("dp"),
        P("dp", "tensor"),
        P("dp"),
        P("tensor", "dp"),
        P("dp"),
        P("tensor", "dp", None),
    )
    return jax.shard_map(
        body,
        mesh=mesh,
        in_specs=placed,
        out_specs=(
            P("tensor", "dp", None),
            P("tensor", "dp", None),
            P("dp"),
            P("dp"),
            P(None, "dp", "tensor"),
            P(None, "dp"),
            P("tensor", "dp"),
            P("dp"),
            P("dp"),
            P("dp"),
            P("dp", "tensor"),
            P("dp"),
            P("tensor", "dp"),
            P("dp"),
        ),
        check_vma=False,
    )
```
